512 devices in a mesh: dp: 64 (over x, z, core), tensor: 8 (over y).
Axes of the slice: x: 4, y: 8, z: 8, core: 2. Of those that a mesh axis runs over, the one named last changes fastest.
Arguments:
- token_ids: int32 [2, 128, 64], P(None, 'dp'), may hold values from 0 to 250111
- lengths: int32 [2, 128], P(None, 'dp'), may hold values from 8 to 64, as said below
- positives: int32 [128], P('dp'), may hold values from 0 to 127, each once
- embed_table: bfloat16 [2048, 250112], P('dp', 'tensor'), may hold values from -6 to 6
- norm_gain: float32 [2048], replicated, may hold values from 0.3 to 3
- w_gate: bfloat16 [2048, 3072], P('dp', 'tensor'), may hold values from -0.125 to 0.125
- w_up: bfloat16 [2048, 3072], P('dp', 'tensor'), may hold values from -0.125 to 0.125
- w_down: bfloat16 [3072, 2048], P('tensor', 'dp'), may hold values from -0.109375 to 0.109375
Outputs:
- loss: float32 [], replicated
- grad_up: float32 [2048, 3072], P('dp', 'tensor')
The draws below stay inside these ranges and needn't reach their ends.
Inputs may be any that keep to these rules, and one draw needn't show every extreme that they name: `lengths`: each query and passage has at least 8 real tokens; some has 64, some has 8. `positives`: every passage is the positive of exactly one query.
All inputs are finite; a program needn't handle non-finite values.
Results may differ from the reference program's by a relative error of at most 0.008.
Values may be sent and summed in bfloat16 or wider, within the bound.
No kernel may reach another device: no remote copies, remote signals or barrier semaphores. Data moves between devices by JAX's collectives and lax.ppermute only.
A program may use at most 64 MiB of HBM per device.

```python
import math
import jax
import jax.numpy as jnp
import numpy as np
from jax import lax

D = 2048
VOCAB = 250112
FF = 3072
LEN = 64
PAIRS = 128


def draw_lengths(key, part):
    key = jax.random.fold_in(key, 11)
    first, second, third = jax.random.split(key, 3)
    counts = jax.random.randint(first, (2, PAIRS), LEN // 8, LEN + 1, dtype=jnp.int32)
    longest = jax.random.randint(second, (), 0, PAIRS, dtype=jnp.int32)
    shortest = jax.random.randint(third, (), 0, PAIRS, dtype=jnp.int32)
    counts = counts.at[0, longest].set(LEN)
    counts = counts.at[1, shortest].set(LEN // 8)
    return counts


def plant(entries, key, least, largest):
    longest = entries.shape.index(max(entries.shape))
    spots = []
    for shift in (0, 1):
        where = [jax.random.randint(jax.random.fold_in(key, axis), (), 0, length) for axis, length in enumerate(entries.shape)]
        where[longest] = (where[longest] + shift) % entries.shape[longest]
        spots.append(tuple(where))
    return entries.at[spots[0]].set(least).at[spots[1]].set(largest)


def steps_of(stream_key, shape, pieces, least, top_value):
    factor_of, own = 1.0, jax.random.fold_in(stream_key, 6)
    for position, parts in pieces:
        heights = jnp.exp(jax.random.uniform(jax.random.fold_in(own, position), (parts,), jnp.float32, least / len(pieces), top_value / len(pieces)))
        factor_of = factor_of * jnp.repeat(heights, shape[position] // parts).reshape([-1 if axis == position else 1 for axis in range(len(shape))])
    return factor_of


def wide_ids(stream_key, shape, amount, slope):
    weights = [min(1 << octave, amount + 1 - (1 << octave)) * (1 << 20) // math.isqrt((1 << octave) ** slope) + 1 for octave in range((amount + 1).bit_length()) if 1 << octave <= amount]
    deviation = 1 + sum(weights) // (1 << 30)
    table = np.cumsum(np.array([max(1, weight // deviation) for weight in weights]))
    ticket = jax.random.randint(jax.random.fold_in(stream_key, 1), shape, 0, int(table[len(weights) - 1]))
    start = jnp.left_shift(1, jnp.searchsorted(jnp.asarray(table, jnp.int32), ticket, side="right").astype(jnp.int32))
    standing = start - 1 + jax.random.randint(jax.random.fold_in(stream_key, 4), shape, 0, 1 << 30) % jnp.minimum(start, amount + 1 - start)
    return jax.random.permutation(jax.random.fold_in(stream_key, 2), amount)[standing].astype(jnp.int32)


def bell_draw(stream_key, shape, spread, reach, cuts=(), held_as=jnp.bfloat16):
    gain = steps_of(stream_key, shape, cuts, -0.22, 0.18) if cuts else 1.0
    result = jax.random.normal(stream_key, shape, jnp.float32) * spread * gain
    return jnp.minimum(jnp.maximum(result, -reach), reach).astype(held_as)


def setup_inputs(seed: int = 0) -> dict:
    key_list = jax.random.split(jax.random.key(seed), 9)
    token_ids = plant(wide_ids(key_list[0], (2, PAIRS, LEN), VOCAB, 2), jax.random.fold_in(key_list[0], 3), 0, VOCAB - 1).astype(jnp.int32)
    lengths = draw_lengths(jax.random.fold_in(key_list[8], 71), 0)
    positives = jax.random.permutation(key_list[2], PAIRS).astype(jnp.int32)
    embed_table = bell_draw(key_list[3], (D, VOCAB), 1.0, 6.0, ((0, 64), (1, 8)))
    norm_gain = jnp.clip(jnp.exp(jax.random.uniform(key_list[4], (D,), jnp.float32, math.log(0.3), math.log(3.0))), 0.3, 3.0)
    w_gate = bell_draw(key_list[5], (D, FF), D ** -0.5, 0.125, ((0, 64), (1, 8)))
    w_up = bell_draw(key_list[6], (D, FF), D ** -0.5, 0.125, ((0, 64), (1, 8)))
    w_down = bell_draw(key_list[7], (FF, D), FF ** -0.5, 0.109375, ((0, 8), (1, 64)))
    return {"token_ids": token_ids, "lengths": lengths, "positives": positives, "embed_table": embed_table, "norm_gain": norm_gain, "w_gate": w_gate, "w_up": w_up, "w_down": w_down}


score_scale = 20.0

def rms_scale(values):
    return lax.rsqrt(lax.optimization_barrier(jnp.mean(values * values, axis=-1, keepdims=True)) + 1e-06)

def product(left, right):
    return jnp.dot(left, right, preferred_element_type=jnp.float32)

def reference(token_ids, lengths, positives, embed_table, norm_gain, w_gate, w_up, w_down):
    flat_ids = token_ids.reshape(-1).astype(jnp.int32)
    embedded = jnp.take(embed_table.T, flat_ids, axis=0)
    resid = embedded.astype(jnp.float32)
    normed = (resid * rms_scale(resid) * norm_gain).astype(jnp.bfloat16)
    gate_proj = product(normed, w_gate)
    up_proj = product(normed, w_up)
    hidden = (jax.nn.gelu(gate_proj, approximate=True) * up_proj).astype(jnp.bfloat16)
    states = resid + product(hidden, w_down)
    positions = jnp.arange(LEN, dtype=jnp.int32)
    pad_mask = (positions[None, None, :] < lengths[:, :, None]).astype(jnp.float32)
    seq_lens = lengths.astype(jnp.float32)
    pooled = jnp.einsum('spt,sptd->spd', pad_mask, states.reshape(2, PAIRS, LEN, D), precision=lax.Precision.HIGHEST) / seq_lens[:, :, None]
    inv_rms = rms_scale(pooled)
    reps = (pooled * inv_rms).astype(jnp.bfloat16)
    factor = score_scale / D
    scores = factor * product(reps[0], reps[1].T)
    log_total = jnp.log(lax.optimization_barrier(jnp.sum(jnp.exp(scores), axis=1)))
    columns = jnp.arange(PAIRS, dtype=jnp.int32)
    one_hot = (columns[None, :] == positives[:, None]).astype(jnp.float32)
    chosen = lax.optimization_barrier(jnp.sum(scores * one_hot, axis=1))
    loss = jnp.sum(log_total - chosen) / PAIRS
    coef = (jnp.exp(scores - log_total[:, None]) - one_hot).astype(jnp.bfloat16)
    grad_query = factor * product(coef, reps[1])
    grad_passage = factor * product(coef.T, reps[0])
    grad_reps = jnp.stack([grad_query, grad_passage])
    grad_pooled = inv_rms * grad_reps - pooled * inv_rms ** 3 * lax.optimization_barrier(jnp.sum(grad_reps * pooled, axis=-1, keepdims=True)) / D
    token_grad = ((grad_pooled / seq_lens[:, :, None])[:, :, None, :] * pad_mask[..., None]).reshape(-1, D).astype(jnp.bfloat16)
    d_hidden = product(token_grad, w_down.T)
    d_up = (d_hidden * jax.nn.gelu(gate_proj, approximate=True)).astype(jnp.bfloat16)
    grad_up = product(normed.T, d_up)
    return (loss, grad_up)
```

```python
import jax
import jax.numpy as jnp
from jax import lax
from jax.sharding import PartitionSpec as P

score_scale = 20.0


def product(left, right, left_dim, right_dim):
    return lax.dot_general(
        left, right, (((left_dim,), (right_dim,)), ((), ())), preferred_element_type=jnp.float32
    )


def gather_all(block, axis):
    count = lax.axis_size(axis)
    copies = jnp.broadcast_to(block[None], (count,) + block.shape)
    return lax.all_to_all(copies, axis, 0, 0, tiled=True)


def on_device(token_ids, lengths, positives, embed_table, norm_gain, w_gate, w_up, w_down):
    dp_count = lax.axis_size("dp")
    tensor_count = lax.axis_size("tensor")
    pair_dev = token_ids.shape[1]
    seq_len = token_ids.shape[2]
    feats, vocab_block = embed_table.shape
    width = feats * dp_count
    units = w_gate.shape[1]
    pair_total = pair_dev * dp_count
    tokens = 2 * pair_dev * seq_len
    part = feats // tensor_count

    with jax.named_scope("weights"):
        rows = jnp.concatenate([w_gate, w_up, w_down.T], axis=1)
        weights = lax.all_gather(rows, "dp", axis=0, tiled=True)

    with jax.named_scope("ids"):
        flat = jnp.concatenate([token_ids.reshape(-1), positives])
        flat = jnp.pad(flat, (0, -flat.shape[0] % 128)).reshape(-1, 128)
        arrived = gather_all(flat, "dp").reshape(dp_count, -1)
        all_ids = arrived[:, :tokens]
        all_pos = arrived[:, tokens : tokens + pair_dev].reshape(-1)

    with jax.named_scope("lookup"):
        local_ids = all_ids.reshape(-1) - lax.axis_index("tensor") * vocab_block
        inside = (local_ids >= 0) & (local_ids < vocab_block)
        safe_ids = jnp.clip(local_ids, 0, vocab_block - 1)
        picked = jnp.take(embed_table, safe_ids, axis=1)
        picked = jnp.where(inside[None, :], picked, jnp.zeros((), picked.dtype))

    with jax.named_scope("embed_exchange"):
        blocks = picked.reshape(tensor_count, part, dp_count, tokens).transpose(2, 0, 1, 3)
        blocks = blocks.reshape(dp_count * tensor_count, part, tokens)
        blocks = lax.all_to_all(blocks, ("dp", "tensor"), 0, 0, tiled=True)
        blocks = blocks.reshape(dp_count, tensor_count, part, tokens)
        mine = jnp.sum(blocks.astype(jnp.float32), axis=1).astype(jnp.bfloat16)
        mine = mine.reshape(dp_count * part, tokens)
        full = gather_all(mine, "tensor").reshape(tensor_count, dp_count, part, tokens)
        embedded = full.transpose(1, 0, 2, 3).reshape(width, tokens)

    with jax.named_scope("forward"):
        resid = embedded.astype(jnp.float32)
        scale = lax.rsqrt(jnp.mean(resid * resid, axis=0, keepdims=True) + 1e-06)
        normed = (resid * scale * norm_gain[:, None]).astype(jnp.bfloat16)
        gate_proj = product(weights[:, :units], normed, 0, 0)
        up_proj = product(weights[:, units : 2 * units], normed, 0, 0)
        down = weights[:, 2 * units :]
        activated = jax.nn.gelu(gate_proj, approximate=True)
        hidden = (activated * up_proj).astype(jnp.bfloat16)

    with jax.named_scope("pool"):
        seq_lens = lengths.reshape(-1).astype(jnp.float32)
        positions = jnp.arange(seq_len, dtype=jnp.int32)
        pad_mask = (positions[None, :] < lengths.reshape(-1)[:, None]).astype(jnp.float32)
        sentences = 2 * pair_dev
        hidden_sum = jnp.sum(
            hidden.astype(jnp.float32).reshape(units, sentences, seq_len) * pad_mask[None], axis=2
        )
        resid_sum = jnp.sum(resid.reshape(width, sentences, seq_len) * pad_mask[None], axis=2)
        high = hidden_sum.astype(jnp.bfloat16)
        low = (hidden_sum - high.astype(jnp.float32)).astype(jnp.bfloat16)
        both = product(jnp.concatenate([high, low], axis=1), down, 0, 1)
        partial_out = both[:sentences] + both[sentences:]
        out_sum = jnp.sum(gather_all(partial_out, "tensor"), axis=0)
        pooled = (resid_sum.T + out_sum) / seq_lens[:, None]
        inv_rms = lax.rsqrt(jnp.mean(pooled * pooled, axis=-1, keepdims=True) + 1e-06)
        reps = (pooled * inv_rms).astype(jnp.bfloat16)

    with jax.named_scope("scores"):
        all_reps = gather_all(reps, "dp")
        queries = all_reps[:, :pair_dev].reshape(pair_total, width)
        passages = all_reps[:, pair_dev:].reshape(pair_total, width)
        factor = score_scale / width
        scores = factor * product(queries, passages, 1, 1)
        log_total = jnp.log(jnp.sum(jnp.exp(scores), axis=1, keepdims=True))
        columns = jnp.arange(pair_total, dtype=jnp.int32)
        one_hot = (columns[None, :] == all_pos[:, None]).astype(jnp.float32)
        chosen = jnp.sum(scores * one_hot, axis=1, keepdims=True)
        loss = jnp.sum(log_total - chosen) / pair_total
        coef = (jnp.exp(scores - log_total) - one_hot).astype(jnp.bfloat16)
        first = lax.axis_index("dp") * pair_dev
        coef_rows = lax.dynamic_slice_in_dim(coef, first, pair_dev, 0)
        coef_columns = lax.dynamic_slice_in_dim(coef, first, pair_dev, 1)
        grad_query = factor * product(coef_rows, passages, 1, 0)
        grad_passage = factor * product(coef_columns, queries, 0, 0)

    with jax.named_scope("backward"):
        grad_reps = jnp.concatenate([grad_query, grad_passage])
        grad_pooled = (
            inv_rms * grad_reps
            - pooled * inv_rms**3 * jnp.sum(grad_reps * pooled, axis=-1, keepdims=True) / width
        )
        token_grad = (grad_pooled / seq_lens[:, None]).astype(jnp.bfloat16)
        d_hidden = product(down, token_grad, 0, 1)
        d_tokens = (d_hidden[:, :, None] * pad_mask[None]).reshape(units, tokens)
        d_up = (d_tokens * activated).astype(jnp.bfloat16)
        partial_grad = product(normed, d_up, 1, 1).astype(jnp.bfloat16)
        parts = lax.all_to_all(
            partial_grad.reshape(dp_count, feats, units), "dp", 0, 0, tiled=True
        )
        grad_up = jnp.sum(parts.astype(jnp.float32), axis=0)
    return (loss, grad_up)


def solution(mesh):
    in_specs = (
        P(None, "dp", None),
        P(None, "dp"),
        P("dp"),
        P("dp", "tensor"),
        P(),
        P("dp", "tensor"),
        P("dp", "tensor"),
        P("tensor", "dp"),
    )
    out_specs = (P(), P("dp", "tensor"))
    return jax.shard_map(
        on_device, mesh=mesh, in_specs=in_specs, out_specs=out_specs, check_vma=False
    )
```

```python
import functools

import jax
import jax.numpy as jnp
from jax import lax
from jax.experimental import pallas as pl
from jax.experimental.pallas import tpu as pltpu
from jax.sharding import PartitionSpec as P

score_scale = 20.0
lanes = 128


def product(left, right, left_dim, right_dim):
    return lax.dot_general(
        left, right, (((left_dim,), (right_dim,)), ((), ())), preferred_element_type=jnp.float32
    )


def gather_all(block, axis):
    count = lax.axis_size(axis)
    copies = jnp.broadcast_to(block[None], (count,) + block.shape)
    return lax.all_to_all(copies, axis, 0, 0, tiled=True)


def pack_kernel(span, table_ref, rows_ref):
    feats, vocab = table_ref.shape
    slots = lanes // feats

    def piece(slot, start, wide):
        return table_ref[:, pl.ds(slot * span + start, wide)].astype(jnp.float32)

    whole = (vocab - (slots - 1) * span) // lanes

    @pl.loop(0, whole)
    def _(step):
        start = pl.multiple_of(step * lanes, lanes)
        stacked = jnp.concatenate([piece(slot, start, lanes) for slot in range(slots)], axis=0)
        rows_ref[pl.ds(start, lanes), :] = stacked.T

    for step in range(whole, span // lanes):
        start = step * lanes
        left = max(0, vocab - (slots - 1) * span - start)
        last = jnp.zeros((feats, lanes - left), jnp.float32)
        if left:
            last = jnp.concatenate([piece(slots - 1, start, left), last], axis=1)
        stacked = jnp.concatenate([piece(slot, start, lanes) for slot in range(slots - 1)] + [last], axis=0)
        rows_ref[start : start + lanes, :] = stacked.T


def pick_kernel(row_ref, slot_ref, rows_ref, out_ref, held_ref):
    groups, tokens = row_ref.shape
    feats = out_ref.shape[1]
    slots = lanes // feats

    @pl.loop(0, groups)
    def _(group):
        for token in range(tokens):
            held_ref[pl.ds(token, 1), :] = rows_ref[pl.ds(row_ref[group, token], 1), :]
        slot = slot_ref[pl.ds(group, 1), :]
        for first in range(0, tokens, lanes):
            turned = held_ref[first : first + lanes, :].T
            mine = slot[:, first : first + lanes]
            total = jnp.zeros((feats, lanes), jnp.float32)
            for index in range(slots):
                total += jnp.where(mine == index, turned[index * feats : (index + 1) * feats], 0.0)
            out_ref[group, :, first : first + lanes] = total.astype(out_ref.dtype)


def pack_table(table):
    feats, vocab = table.shape
    slots = lanes // feats
    span = -(-vocab // (slots * lanes)) * lanes
    return pl.pallas_call(
        functools.partial(pack_kernel, span),
        out_shape=jax.ShapeDtypeStruct((span, lanes), jnp.float32),
        in_specs=[pl.BlockSpec(memory_space=pltpu.VMEM)],
        out_specs=pl.BlockSpec(memory_space=pltpu.VMEM),
        compiler_params=pltpu.CompilerParams(vmem_limit_bytes=32 << 20),
        cost_estimate=pl.CostEstimate(flops=0, bytes_accessed=3 * feats * vocab * 2, transcendentals=0),
    )(table)


def pick_rows(rows, packed, feats):
    slots = lanes // feats
    span = packed.shape[0]
    groups, tokens = rows.shape
    inside = (rows >= 0) & (rows < slots * span)
    safe = jnp.where(inside, rows, 0)
    slot = safe // span
    row = safe - slot * span
    slot = jnp.where(inside, slot, slots)
    return pl.pallas_call(
        pick_kernel,
        out_shape=jax.ShapeDtypeStruct((groups, feats, tokens), jnp.bfloat16),
        in_specs=[
            pl.BlockSpec(memory_space=pltpu.SMEM),
            pl.BlockSpec(memory_space=pltpu.VMEM),
            pl.BlockSpec(memory_space=pltpu.VMEM),
        ],
        out_specs=pl.BlockSpec(memory_space=pltpu.VMEM),
        scratch_shapes=[pltpu.VMEM((tokens, lanes), jnp.float32)],
        compiler_params=pltpu.CompilerParams(vmem_limit_bytes=32 << 20),
        cost_estimate=pl.CostEstimate(flops=0, bytes_accessed=30 << 20, transcendentals=0),
    )(row, slot, packed)


def on_device(token_ids, lengths, positives, embed_table, norm_gain, w_gate, w_up, w_down):
    dp_count = lax.axis_size("dp")
    tensor_count = lax.axis_size("tensor")
    pair_dev = token_ids.shape[1]
    seq_len = token_ids.shape[2]
    feats, vocab_block = embed_table.shape
    width = feats * dp_count
    units = w_gate.shape[1]
    pair_total = pair_dev * dp_count
    tokens = 2 * pair_dev * seq_len
    part = feats // tensor_count
    even_core = lax.axis_index("dp") % 2 == 0
    swap_cores = [(index, index ^ 1) for index in range(dp_count)]

    with jax.named_scope("weights"):
        rows = jnp.concatenate([w_gate, w_up, w_down.T], axis=1)
        weights = lax.all_gather(rows, "dp", axis=0, tiled=True)

    with jax.named_scope("ids"):
        flat = jnp.concatenate([token_ids.reshape(-1), positives])
        flat = jnp.pad(flat, (0, -flat.shape[0] % 128)).reshape(-1, 128)
        arrived = gather_all(flat, "dp").reshape(dp_count, -1)
        all_ids = arrived[:, :tokens]
        all_pos = arrived[:, tokens : tokens + pair_dev].reshape(-1)

    with jax.named_scope("lookup"):
        local_ids = all_ids - lax.axis_index("tensor") * vocab_block
        inside = (local_ids >= 0) & (local_ids < vocab_block)
        picked = pick_rows(jnp.where(inside, local_ids, -1), pack_table(embed_table), feats)

    with jax.named_scope("embed_exchange"):
        blocks = picked.reshape(dp_count * tensor_count, part, tokens)
        blocks = lax.all_to_all(blocks, ("dp", "tensor"), 0, 0, tiled=True)
        blocks = blocks.reshape(dp_count, tensor_count, part, tokens)
        mine = jnp.sum(blocks.astype(jnp.float32), axis=1).astype(jnp.bfloat16)
        mine = mine.reshape(dp_count * part, tokens)
        full = gather_all(mine, "tensor").reshape(tensor_count, dp_count, part, tokens)
        embedded = full.transpose(1, 0, 2, 3).reshape(width, tokens)

    with jax.named_scope("forward"):
        resid = embedded.astype(jnp.float32)
        scale = lax.rsqrt(jnp.mean(resid * resid, axis=0, keepdims=True) + 1e-06)
        normed = (resid * scale * norm_gain[:, None]).astype(jnp.bfloat16)
        gate_proj = product(weights[:, :units], normed, 0, 0)
        up_proj = product(weights[:, units : 2 * units], normed, 0, 0)
        down = weights[:, 2 * units :]
        activated = jax.nn.gelu(gate_proj, approximate=True)
        hidden = lax.reduce_precision(activated * up_proj, 8, 7)

    with jax.named_scope("pool"):
        seq_lens = lengths.reshape(-1).astype(jnp.float32)
        positions = jnp.arange(seq_len, dtype=jnp.int32)
        pad_mask = (positions[None, :] < lengths.reshape(-1)[:, None]).astype(jnp.float32)
        sentences = 2 * pair_dev
        hidden_sum = jnp.sum(
            hidden.reshape(units, sentences, seq_len) * pad_mask[None], axis=2
        )
        resid_sum = jnp.sum(resid.reshape(width, sentences, seq_len) * pad_mask[None], axis=2)
        high = lax.reduce_precision(hidden_sum, 8, 7)
        terms = jnp.concatenate([high, hidden_sum - high], axis=1).astype(jnp.bfloat16)
        both = product(terms, down, 0, 1)
        partial_out = both[:sentences] + both[sentences:]
        out_sum = jnp.sum(gather_all(partial_out, "tensor"), axis=0)
        pooled = (resid_sum.T + out_sum) / seq_lens[:, None]
        inv_rms = lax.rsqrt(jnp.mean(pooled * pooled, axis=-1, keepdims=True) + 1e-06)
        reps = (pooled * inv_rms).astype(jnp.bfloat16)

    with jax.named_scope("scores"):
        half = width // 2
        halves = reps.reshape(2 * pair_dev, 2, half).transpose(1, 0, 2)
        halves = jnp.broadcast_to(halves[None], (dp_count // 2, 2, 2 * pair_dev, half))
        mine = lax.all_to_all(
            halves.reshape(dp_count, 2 * pair_dev, half), "dp", 0, 0, tiled=True
        )
        sides = [mine, lax.ppermute(mine, "dp", swap_cores)]
        queries = [side[:, :pair_dev].reshape(pair_total, half) for side in sides]
        passages = [side[:, pair_dev:].reshape(pair_total, half) for side in sides]
        factor = score_scale / width
        scores = factor * sum(product(q, p, 1, 1) for q, p in zip(queries, passages))
        log_total = jnp.log(jnp.sum(jnp.exp(scores), axis=1, keepdims=True))
        columns = jnp.arange(pair_total, dtype=jnp.int32)
        one_hot = (columns[None, :] == all_pos[:, None]).astype(jnp.float32)
        chosen = jnp.sum(scores * one_hot, axis=1, keepdims=True)
        loss = jnp.sum(log_total - chosen) / pair_total
        coef = (jnp.exp(scores - log_total) - one_hot).astype(jnp.bfloat16)
        first = lax.axis_index("dp") * pair_dev
        coef_rows = lax.dynamic_slice_in_dim(coef, first, pair_dev, 0)
        coef_columns = lax.dynamic_slice_in_dim(coef, first, pair_dev, 1)
        grads = [
            factor * jnp.concatenate([product(coef_rows, p, 1, 0), product(coef_columns, q, 0, 0)])
            for q, p in zip(queries, passages)
        ]
        grad_reps = jnp.where(
            even_core,
            jnp.concatenate([grads[0], grads[1]], axis=1),
            jnp.concatenate([grads[1], grads[0]], axis=1),
        )

    with jax.named_scope("backward"):
        grad_pooled = (
            inv_rms * grad_reps
            - pooled * inv_rms**3 * jnp.sum(grad_reps * pooled, axis=-1, keepdims=True) / width
        )
        token_grad = (grad_pooled / seq_lens[:, None]).astype(jnp.bfloat16)
        d_hidden = product(down, token_grad, 0, 1)
        d_tokens = (d_hidden[:, :, None] * pad_mask[None]).reshape(units, tokens)
        d_up = (d_tokens * activated).astype(jnp.bfloat16)
        by_core = normed.reshape(dp_count // 2, 2, feats, tokens)
        own_rows = jnp.where(even_core, by_core[:, 0], by_core[:, 1]).reshape(-1, tokens)
        other_rows = jnp.where(even_core, by_core[:, 1], by_core[:, 0]).reshape(-1, tokens)
        sent = product(other_rows, d_up, 1, 1).astype(jnp.bfloat16)
        got = lax.ppermute(sent, "dp", swap_cores)
        partial_grad = (product(own_rows, d_up, 1, 1) + got.astype(jnp.float32)).astype(jnp.bfloat16)
        same_core = [list(range(core, dp_count, 2)) for core in range(2)]
        parts = lax.all_to_all(
            partial_grad.reshape(dp_count // 2, feats, units),
            "dp",
            0,
            0,
            tiled=True,
            axis_index_groups=same_core,
        )
        grad_up = jnp.sum(parts.astype(jnp.float32), axis=0)
    return (loss, grad_up)


def solution(mesh):
    in_specs = (
        P(None, "dp", None),
        P(None, "dp"),
        P("dp"),
        P("dp", "tensor"),
        P(),
        P("dp", "tensor"),
        P("dp", "tensor"),
        P("tensor", "dp"),
    )
    out_specs = (P(), P("dp", "tensor"))
    return jax.shard_map(
        on_device, mesh=mesh, in_specs=in_specs, out_specs=out_specs, check_vma=False
    )
```

```python
import functools

import jax
import jax.numpy as jnp
from jax import lax
from jax.experimental import pallas as pl
from jax.experimental.pallas import tpu as pltpu
from jax.sharding import PartitionSpec as P

score_scale = 20.0
lanes = 128


def product(left, right, left_dim, right_dim):
    return lax.dot_general(
        left, right, (((left_dim,), (right_dim,)), ((), ())), preferred_element_type=jnp.float32
    )


def gather_all(block, axis):
    count = lax.axis_size(axis)
    copies = jnp.broadcast_to(block[None], (count,) + block.shape)
    return lax.all_to_all(copies, axis, 0, 0, tiled=True)


def ids_kernel(pos_ref, ids_ref, out_ref):
    sides, pair_dev, seq_len = ids_ref.shape
    ids = jnp.concatenate(
        [ids_ref[side, pl.ds(pair, 1), :] for side in range(sides) for pair in range(pair_dev)], axis=1
    )
    lane = lax.broadcasted_iota(jnp.int32, (1, lanes), 1)
    marks = jnp.zeros((1, lanes), jnp.int32)
    for pair in range(pair_dev):
        marks = jnp.where(lane == pair, pos_ref[pair], marks)
    rows = [ids[:, start : start + lanes] for start in range(0, ids.shape[1], lanes)] + [marks]
    out_ref[...] = jnp.broadcast_to(jnp.concatenate(rows, axis=0)[None], out_ref.shape)


def spread_ids(token_ids, positives, count):
    return pl.pallas_call(
        ids_kernel,
        out_shape=jax.ShapeDtypeStruct((count, token_ids.size // lanes + 1, lanes), jnp.int32),
        in_specs=[pl.BlockSpec(memory_space=pltpu.SMEM), pl.BlockSpec(memory_space=pltpu.VMEM)],
        out_specs=pl.BlockSpec(memory_space=pltpu.VMEM),
    )(positives, token_ids)


def pack_kernel(span, table_ref, rows_ref):
    feats, vocab = table_ref.shape
    slots = lanes // feats

    def piece(slot, start, wide):
        return table_ref[:, pl.ds(slot * span + start, wide)].astype(jnp.float32)

    whole = (vocab - (slots - 1) * span) // lanes

    @pl.loop(0, whole)
    def _(step):
        start = pl.multiple_of(step * lanes, lanes)
        stacked = jnp.concatenate([piece(slot, start, lanes) for slot in range(slots)], axis=0)
        rows_ref[pl.ds(start, lanes), 0, :] = stacked.T

    for step in range(whole, span // lanes):
        start = step * lanes
        left = max(0, vocab - (slots - 1) * span - start)
        last = jnp.zeros((feats, lanes - left), jnp.float32)
        if left:
            last = jnp.concatenate([piece(slots - 1, start, left), last], axis=1)
        stacked = jnp.concatenate([piece(slot, start, lanes) for slot in range(slots - 1)] + [last], axis=0)
        rows_ref[start : start + lanes, 0, :] = stacked.T


def pick_kernel(chunks, row_ref, slot_ref, rows_ref, out_ref, even_ref, odd_ref, near_ref, sems):
    groups, tokens = row_ref.shape
    feats = out_ref.shape[1]
    slots = lanes // feats
    chunk = groups // chunks

    def bring(index):
        where = pl.ds(index * chunk, chunk)
        return pltpu.make_async_copy(row_ref.at[where], near_ref.at[where], sems.at[index])

    def read(group, held_ref):
        for token in range(tokens):
            held_ref[pl.ds(token, 1), :] = rows_ref[near_ref[group, token]]

    def turn(group, held_ref):
        slot = slot_ref[pl.ds(group, 1), :]
        for first in range(0, tokens, lanes):
            turned = held_ref[first : first + lanes, :].T
            mine = slot[:, first : first + lanes]
            total = jnp.zeros((feats, lanes), jnp.float32)
            for part in range(slots):
                total = jnp.where(mine == part, turned[part * feats : (part + 1) * feats], total)
            out_ref[group, :, first : first + lanes] = total.astype(out_ref.dtype)

    for index in range(chunks):
        bring(index).start()
    bring(0).wait()
    read(0, even_ref)

    @pl.loop(0, groups // 2)
    def _(step):
        ahead = step * 2 // chunk + 1

        @pl.when((step * 2 % chunk == 0) & (ahead < chunks))
        def _():
            bring(ahead).wait()

        read(step * 2 + 1, odd_ref)
        turn(step * 2, even_ref)
        read(jnp.minimum(step * 2 + 2, groups - 1), even_ref)
        turn(step * 2 + 1, odd_ref)


def pack_table(table):
    feats, vocab = table.shape
    slots = lanes // feats
    span = -(-vocab // (slots * lanes)) * lanes
    return pl.pallas_call(
        functools.partial(pack_kernel, span),
        out_shape=jax.ShapeDtypeStruct((span, 1, lanes), jnp.float32),
        in_specs=[pl.BlockSpec(memory_space=pltpu.VMEM)],
        out_specs=pl.BlockSpec(memory_space=pltpu.VMEM),
        compiler_params=pltpu.CompilerParams(vmem_limit_bytes=32 << 20),
        cost_estimate=pl.CostEstimate(flops=0, bytes_accessed=20 << 20, transcendentals=0),
    )(table)


def pick_rows(rows, packed, feats):
    slots = lanes // feats
    span = packed.shape[0]
    groups, tokens = rows.shape
    chunks = 8 if groups % 16 == 0 else 1
    inside = (rows >= 0) & (rows < slots * span)
    safe = jnp.where(inside, rows, 0)
    slot = safe // span
    row = safe - slot * span
    slot = jnp.where(inside, slot, slots)
    return pl.pallas_call(
        functools.partial(pick_kernel, chunks),
        out_shape=jax.ShapeDtypeStruct((groups, feats, tokens), jnp.bfloat16),
        in_specs=[pl.BlockSpec(memory_space=pltpu.VMEM)] * 3,
        out_specs=pl.BlockSpec(memory_space=pltpu.VMEM),
        scratch_shapes=[
            pltpu.VMEM((tokens, lanes), jnp.float32),
            pltpu.VMEM((tokens, lanes), jnp.float32),
            pltpu.SMEM((groups, tokens), jnp.int32),
            pltpu.SemaphoreType.DMA((chunks,)),
        ],
        compiler_params=pltpu.CompilerParams(vmem_limit_bytes=32 << 20),
        cost_estimate=pl.CostEstimate(flops=0, bytes_accessed=30 << 20, transcendentals=0),
    )(row, slot, packed)


def gelu(v):
    return 0.5 * v * (1.0 + jnp.tanh(0.7978845608028654 * (v + 0.044715 * (v * v * v))))


def forward_kernel(units, x_ref, gain_ref, mask_ref, weights_ref, normed_ref, act_ref, out_ref, sum_ref):
    width, tokens = x_ref.shape
    resid = x_ref[...].astype(jnp.float32)
    scale = lax.rsqrt(jnp.mean(resid * resid, axis=0, keepdims=True) + 1e-06)
    normed_ref[...] = (resid * scale * gain_ref[...]).astype(jnp.bfloat16)
    first = (((0,), (0,)), ((), ()))
    both = lax.dot_general(
        normed_ref[...], weights_ref[:, : 2 * units], first, preferred_element_type=jnp.float32
    )
    act = gelu(both[:, :units])
    act_ref[...] = act
    hidden = (act * both[:, units:]).astype(jnp.bfloat16)
    mask = mask_ref[...]
    hidden_sum = jnp.dot(mask, hidden, preferred_element_type=jnp.float32)
    high = hidden_sum.astype(jnp.bfloat16)
    low = (hidden_sum - high.astype(jnp.float32)).astype(jnp.bfloat16)
    last = (((1,), (1,)), ((), ()))
    down = weights_ref[:, 2 * units :]
    terms = lax.dot_general(
        jnp.concatenate([high, low], axis=0), down, last, preferred_element_type=jnp.float32
    )
    rows = mask.shape[0]
    total = terms[:rows] + terms[rows:]
    out_ref[...] = jnp.broadcast_to(total[: out_ref.shape[1]][None], out_ref.shape)
    sum_ref[...] = lax.dot_general(mask, x_ref[...], last, preferred_element_type=jnp.float32)[: sum_ref.shape[0]]


def forward(embedded, gain, mask, weights, units, count, sentences):
    width, tokens = embedded.shape
    return pl.pallas_call(
        functools.partial(forward_kernel, units),
        out_shape=[
            jax.ShapeDtypeStruct((width, tokens), jnp.bfloat16),
            jax.ShapeDtypeStruct((tokens, units), jnp.float32),
            jax.ShapeDtypeStruct((count, sentences, width), jnp.float32),
            jax.ShapeDtypeStruct((sentences, width), jnp.float32),
        ],
        in_specs=[pl.BlockSpec(memory_space=pltpu.VMEM)] * 4,
        out_specs=[pl.BlockSpec(memory_space=pltpu.VMEM)] * 4,
        compiler_params=pltpu.CompilerParams(vmem_limit_bytes=40 << 20),
        cost_estimate=pl.CostEstimate(flops=3 * 2 * width * tokens * units, bytes_accessed=10 << 20, transcendentals=tokens * units),
    )(embedded, gain, mask, weights)


def on_device(token_ids, lengths, positives, embed_table, norm_gain, w_gate, w_up, w_down):
    dp_count = lax.axis_size("dp")
    tensor_count = lax.axis_size("tensor")
    pair_dev = token_ids.shape[1]
    seq_len = token_ids.shape[2]
    feats, vocab_block = embed_table.shape
    width = feats * dp_count
    units = w_gate.shape[1]
    pair_total = pair_dev * dp_count
    tokens = 2 * pair_dev * seq_len
    part = feats // tensor_count
    even_core = lax.axis_index("dp") % 2 == 0
    swap_cores = [(index, index ^ 1) for index in range(dp_count)]

    with jax.named_scope("ids"):
        spread = spread_ids(token_ids, positives, dp_count)
        spread, w_gate, w_up, w_down = lax.optimization_barrier((spread, w_gate, w_up, w_down))
        arrived = lax.all_to_all(spread, "dp", 0, 0, tiled=True)
        all_ids = arrived[:, : tokens // lanes].reshape(dp_count, tokens)
        all_pos = arrived[:, tokens // lanes, :pair_dev].reshape(-1)

    with jax.named_scope("weights"):
        def by_part(rows):
            rows = rows.reshape((dp_count, tensor_count, part) + rows.shape[1:])
            return jnp.swapaxes(rows, 0, 1).reshape((width,) + rows.shape[3:])

        rows = jnp.concatenate([w_gate, w_up, w_down.T], axis=1)
        weights = by_part(lax.all_gather(rows, "dp", axis=0, tiled=True))
        gain = by_part(norm_gain[:, None])

    with jax.named_scope("lookup"):
        local_ids = all_ids - lax.axis_index("tensor") * vocab_block
        inside = (local_ids >= 0) & (local_ids < vocab_block)
        picked = pick_rows(jnp.where(inside, local_ids, -1), pack_table(embed_table), feats)

    with jax.named_scope("embed_exchange"):
        blocks = picked.reshape(dp_count * tensor_count, part, tokens)
        blocks = lax.all_to_all(blocks, ("dp", "tensor"), 0, 0, tiled=True)
        blocks = blocks.reshape(dp_count, tensor_count, part, tokens)
        mine = jnp.sum(blocks.astype(jnp.float32), axis=1).astype(jnp.bfloat16)
        mine = mine.reshape(dp_count * part, tokens)
        embedded = gather_all(mine, "tensor").reshape(width, tokens)

    with jax.named_scope("forward"):
        sentences = 2 * pair_dev
        positions = jnp.arange(seq_len, dtype=jnp.int32)
        pad_mask = positions[None, :] < lengths.reshape(-1)[:, None]
        chosen_tokens = jnp.eye(16, sentences, dtype=jnp.bool_)[:, :, None] & pad_mask[None]
        chosen_tokens = chosen_tokens.reshape(16, tokens).astype(jnp.bfloat16)
        normed, activated, partial_out, resid_sum = forward(
            embedded, gain, chosen_tokens, weights, units, tensor_count, sentences
        )
        down = weights[:, 2 * units :]

    with jax.named_scope("pool"):
        seq_lens = lengths.reshape(-1).astype(jnp.float32)
        out_sum = jnp.sum(lax.all_to_all(partial_out, "tensor", 0, 0, tiled=True), axis=0)
        pooled = (resid_sum + out_sum) / seq_lens[:, None]
        inv_rms = lax.rsqrt(jnp.mean(pooled * pooled, axis=-1, keepdims=True) + 1e-06)
        reps = (pooled * inv_rms).astype(jnp.bfloat16)

    with jax.named_scope("scores"):
        half = width // 2
        halves = reps.reshape(2 * pair_dev, 2, half).transpose(1, 0, 2)
        halves = jnp.broadcast_to(halves[None], (dp_count // 2, 2, 2 * pair_dev, half))
        mine = lax.all_to_all(
            halves.reshape(dp_count, 2 * pair_dev, half), "dp", 0, 0, tiled=True
        )
        sides = [mine, lax.ppermute(mine, "dp", swap_cores)]
        queries = [side[:, :pair_dev].reshape(pair_total, half) for side in sides]
        passages = [side[:, pair_dev:].reshape(pair_total, half) for side in sides]
        factor = score_scale / width
        scores = factor * sum(product(q, p, 1, 1) for q, p in zip(queries, passages))
        log_total = jnp.log(jnp.sum(jnp.exp(scores), axis=1, keepdims=True))
        columns = jnp.arange(pair_total, dtype=jnp.int32)
        one_hot = (columns[None, :] == all_pos[:, None]).astype(jnp.float32)
        chosen = jnp.sum(scores * one_hot, axis=1, keepdims=True)
        loss = jnp.sum(log_total - chosen) / pair_total
        coef = (jnp.exp(scores - log_total) - one_hot).astype(jnp.bfloat16)
        first = lax.axis_index("dp") * pair_dev
        coef_rows = lax.dynamic_slice_in_dim(coef, first, pair_dev, 0)
        coef_columns = lax.dynamic_slice_in_dim(coef, first, pair_dev, 1)
        grads = [
            factor * jnp.concatenate([product(coef_rows, p, 1, 0), product(coef_columns, q, 0, 0)])
            for q, p in zip(queries, passages)
        ]
        grad_reps = jnp.where(
            even_core,
            jnp.concatenate([grads[0], grads[1]], axis=1),
            jnp.concatenate([grads[1], grads[0]], axis=1),
        )

    with jax.named_scope("backward"):
        grad_pooled = (
            inv_rms * grad_reps
            - pooled * inv_rms**3 * jnp.sum(grad_reps * pooled, axis=-1, keepdims=True) / width
        )
        token_grad = (grad_pooled / seq_lens[:, None]).astype(jnp.bfloat16)
        d_hidden = product(token_grad, down, 1, 0)
        d_tokens = jnp.where(pad_mask[:, :, None], d_hidden[:, None, :], 0.0).reshape(tokens, units)
        d_up = (d_tokens * activated).astype(jnp.bfloat16)
        by_core = normed.reshape(tensor_count, dp_count // 2, 2, part, tokens)
        sides = [jnp.where(even_core == side, by_core[:, :, 0], by_core[:, :, 1]) for side in (True, False)]
        own_rows, other_rows = (jnp.swapaxes(side, 0, 1).reshape(-1, tokens) for side in sides)
        sent = product(other_rows, d_up, 1, 0).astype(jnp.bfloat16)
        got = lax.ppermute(sent, "dp", swap_cores)
        partial_grad = (product(own_rows, d_up, 1, 0) + got.astype(jnp.float32)).astype(jnp.bfloat16)
        same_core = [list(range(core, dp_count, 2)) for core in range(2)]
        parts = lax.all_to_all(
            partial_grad.reshape(dp_count // 2, feats, units),
            "dp",
            0,
            0,
            tiled=True,
            axis_index_groups=same_core,
        )
        grad_up = jnp.sum(parts.astype(jnp.float32), axis=0)
    return (loss, grad_up)


def solution(mesh):
    in_specs = (
        P(None, "dp", None),
        P(None, "dp"),
        P("dp"),
        P("dp", "tensor"),
        P(),
        P("dp", "tensor"),
        P("dp", "tensor"),
        P("tensor", "dp"),
    )
    out_specs = (P(), P("dp", "tensor"))
    return jax.shard_map(
        on_device, mesh=mesh, in_specs=in_specs, out_specs=out_specs, check_vma=False
    )
```

```python
import functools

import jax
import jax.numpy as jnp
from jax import lax
from jax.experimental import pallas as pl
from jax.experimental.pallas import tpu as pltpu
from jax.sharding import PartitionSpec as P

score_scale = 20.0
lanes = 128


def product(left, right, left_dim, right_dim):
    return lax.dot_general(
        left, right, (((left_dim,), (right_dim,)), ((), ())), preferred_element_type=jnp.float32
    )


def gather_all(block, axis):
    count = lax.axis_size(axis)
    copies = jnp.broadcast_to(block[None], (count,) + block.shape)
    return lax.all_to_all(copies, axis, 0, 0, tiled=True)


def ids_kernel(pos_ref, ids_ref, out_ref):
    sides, pair_dev, seq_len = ids_ref.shape
    ids = jnp.concatenate(
        [ids_ref[side, pl.ds(pair, 1), :] for side in range(sides) for pair in range(pair_dev)], axis=1
    )
    lane = lax.broadcasted_iota(jnp.int32, (1, lanes), 1)
    marks = jnp.zeros((1, lanes), jnp.int32)
    for pair in range(pair_dev):
        marks = jnp.where(lane == pair, pos_ref[pair], marks)
    rows = [ids[:, start : start + lanes] for start in range(0, ids.shape[1], lanes)] + [marks]
    out_ref[...] = jnp.broadcast_to(jnp.concatenate(rows, axis=0)[None], out_ref.shape)


def spread_ids(token_ids, positives, count):
    return pl.pallas_call(
        ids_kernel,
        out_shape=jax.ShapeDtypeStruct((count, token_ids.size // lanes + 1, lanes), jnp.int32),
        in_specs=[pl.BlockSpec(memory_space=pltpu.SMEM), pl.BlockSpec(memory_space=pltpu.VMEM)],
        out_specs=pl.BlockSpec(memory_space=pltpu.VMEM),
    )(positives, token_ids)


def pack_kernel(span, table_ref, rows_ref):
    feats, vocab = table_ref.shape
    slots = lanes // feats

    def piece(slot, start, wide):
        return table_ref[:, pl.ds(slot * span + start, wide)].astype(jnp.float32)

    whole = (vocab - (slots - 1) * span) // lanes

    @pl.loop(0, whole)
    def _(step):
        start = pl.multiple_of(step * lanes, lanes)
        stacked = jnp.concatenate([piece(slot, start, lanes) for slot in range(slots)], axis=0)
        rows_ref[pl.ds(start, lanes), 0, :] = stacked.T

    for step in range(whole, span // lanes):
        start = step * lanes
        left = max(0, vocab - (slots - 1) * span - start)
        last = jnp.zeros((feats, lanes - left), jnp.float32)
        if left:
            last = jnp.concatenate([piece(slots - 1, start, left), last], axis=1)
        stacked = jnp.concatenate([piece(slot, start, lanes) for slot in range(slots - 1)] + [last], axis=0)
        rows_ref[start : start + lanes, 0, :] = stacked.T


def pick_kernel(chunks, row_ref, slot_ref, rows_ref, out_ref, even_ref, odd_ref, near_ref, sems):
    groups, tokens = row_ref.shape
    feats = out_ref.shape[1]
    slots = lanes // feats
    chunk = groups // chunks

    def bring(index):
        where = pl.ds(index * chunk, chunk)
        return pltpu.make_async_copy(row_ref.at[where], near_ref.at[where], sems.at[index])

    def read(group, held_ref):
        for token in range(tokens):
            held_ref[pl.ds(token, 1), :] = rows_ref[near_ref[group, token]]

    def turn(group, held_ref):
        slot = slot_ref[pl.ds(group, 1), :]
        for first in range(0, tokens, lanes):
            turned = held_ref[first : first + lanes, :].T
            mine = slot[:, first : first + lanes]
            total = jnp.zeros((feats, lanes), jnp.float32)
            for part in range(slots):
                total = jnp.where(mine == part, turned[part * feats : (part + 1) * feats], total)
            out_ref[group, :, first : first + lanes] = total.astype(out_ref.dtype)

    for index in range(chunks):
        bring(index).start()
    bring(0).wait()
    read(0, even_ref)

    @pl.loop(0, groups // 2)
    def _(step):
        ahead = step * 2 // chunk + 1

        @pl.when((step * 2 % chunk == 0) & (ahead < chunks))
        def _():
            bring(ahead).wait()

        read(step * 2 + 1, odd_ref)
        turn(step * 2, even_ref)
        read(jnp.minimum(step * 2 + 2, groups - 1), even_ref)
        turn(step * 2 + 1, odd_ref)


def pack_table(table):
    feats, vocab = table.shape
    slots = lanes // feats
    span = -(-vocab // (slots * lanes)) * lanes
    return pl.pallas_call(
        functools.partial(pack_kernel, span),
        out_shape=jax.ShapeDtypeStruct((span, 1, lanes), jnp.float32),
        in_specs=[pl.BlockSpec(memory_space=pltpu.VMEM)],
        out_specs=pl.BlockSpec(memory_space=pltpu.VMEM),
        compiler_params=pltpu.CompilerParams(vmem_limit_bytes=10 << 20),
        cost_estimate=pl.CostEstimate(flops=0, bytes_accessed=20 << 20, transcendentals=0),
    )(table)


def pick_rows(rows, packed, feats):
    slots = lanes // feats
    span = packed.shape[0]
    groups, tokens = rows.shape
    chunks = 8 if groups % 16 == 0 else 1
    inside = (rows >= 0) & (rows < slots * span)
    safe = jnp.where(inside, rows, 0)
    slot = safe // span
    row = safe - slot * span
    slot = jnp.where(inside, slot, slots)
    return pl.pallas_call(
        functools.partial(pick_kernel, chunks),
        out_shape=jax.ShapeDtypeStruct((groups, feats, tokens), jnp.bfloat16),
        in_specs=[pl.BlockSpec(memory_space=pltpu.VMEM)] * 3,
        out_specs=pl.BlockSpec(memory_space=pltpu.VMEM),
        scratch_shapes=[
            pltpu.VMEM((tokens, lanes), jnp.float32),
            pltpu.VMEM((tokens, lanes), jnp.float32),
            pltpu.SMEM((groups, tokens), jnp.int32),
            pltpu.SemaphoreType.DMA((chunks,)),
        ],
        compiler_params=pltpu.CompilerParams(vmem_limit_bytes=10 << 20),
        cost_estimate=pl.CostEstimate(flops=0, bytes_accessed=30 << 20, transcendentals=0),
    )(row, slot, packed)


def gelu(v):
    return 0.5 * v * (1.0 + jnp.tanh(0.7978845608028654 * (v + 0.044715 * (v * v * v))))


def forward_kernel(
    units, feats, x_ref, gain_ref, mask_ref, weights_ref, normed_ref, act_ref, out_ref, sum_ref, resid_ref
):
    parts, part_rows, tokens = x_ref.shape
    part = feats // parts
    for index in range(parts):
        rows = x_ref[index].astype(jnp.float32)
        for block in range(part_rows // part):
            start = block * feats + index * part
            resid_ref[start : start + part, :] = rows[block * part : (block + 1) * part]
    resid = resid_ref[...]
    scale = lax.rsqrt(jnp.mean(resid * resid, axis=0, keepdims=True) + 1e-06)
    normed_ref[...] = (resid * scale * gain_ref[...]).astype(jnp.bfloat16)
    first = (((0,), (0,)), ((), ()))
    both = lax.dot_general(
        normed_ref[...], weights_ref[:, : 2 * units], first, preferred_element_type=jnp.float32
    )
    act = gelu(both[:, :units])
    act_ref[...] = act
    hidden = (act * both[:, units:]).astype(jnp.bfloat16)
    mask = mask_ref[...]
    hidden_sum = jnp.dot(mask, hidden, preferred_element_type=jnp.float32)
    high = hidden_sum.astype(jnp.bfloat16)
    low = (hidden_sum - high.astype(jnp.float32)).astype(jnp.bfloat16)
    last = (((1,), (1,)), ((), ()))
    down = weights_ref[:, 2 * units :]
    terms = lax.dot_general(
        jnp.concatenate([high, low], axis=0), down, last, preferred_element_type=jnp.float32
    )
    rows = mask.shape[0]
    total = terms[:rows] + terms[rows:]
    out_ref[...] = jnp.broadcast_to(total[: out_ref.shape[1]][None], out_ref.shape)
    sum_ref[...] = lax.dot_general(
        mask, resid.astype(jnp.bfloat16), last, preferred_element_type=jnp.float32
    )[: sum_ref.shape[0]]


def forward(embedded, gain, mask, weights, units, feats, sentences):
    count, part_rows, tokens = embedded.shape
    width = count * part_rows
    return pl.pallas_call(
        functools.partial(forward_kernel, units, feats),
        out_shape=[
            jax.ShapeDtypeStruct((width, tokens), jnp.bfloat16),
            jax.ShapeDtypeStruct((tokens, units), jnp.float32),
            jax.ShapeDtypeStruct((count, sentences, width), jnp.float32),
            jax.ShapeDtypeStruct((sentences, width), jnp.float32),
        ],
        in_specs=[pl.BlockSpec(memory_space=pltpu.VMEM)] * 4,
        out_specs=[pl.BlockSpec(memory_space=pltpu.VMEM)] * 4,
        scratch_shapes=[pltpu.VMEM((width, tokens), jnp.float32)],
        compiler_params=pltpu.CompilerParams(vmem_limit_bytes=20 << 20),
        cost_estimate=pl.CostEstimate(flops=3 * 2 * width * tokens * units, bytes_accessed=10 << 20, transcendentals=tokens * units),
    )(embedded, gain, mask, weights)


def on_device(token_ids, lengths, positives, embed_table, norm_gain, w_gate, w_up, w_down):
    dp_count = lax.axis_size("dp")
    tensor_count = lax.axis_size("tensor")
    pair_dev = token_ids.shape[1]
    seq_len = token_ids.shape[2]
    feats, vocab_block = embed_table.shape
    width = feats * dp_count
    units = w_gate.shape[1]
    pair_total = pair_dev * dp_count
    tokens = 2 * pair_dev * seq_len
    part = feats // tensor_count
    even_core = lax.axis_index("dp") % 2 == 0
    swap_cores = [(index, index ^ 1) for index in range(dp_count)]

    with jax.named_scope("ids"):
        spread = spread_ids(token_ids, positives, dp_count)
        spread, w_gate, w_up, w_down = lax.optimization_barrier((spread, w_gate, w_up, w_down))
        arrived = lax.all_to_all(spread, "dp", 0, 0, tiled=True)
        all_ids = arrived[:, : tokens // lanes].reshape(dp_count, tokens)
        all_pos = arrived[:, tokens // lanes, :pair_dev].reshape(-1)

    with jax.named_scope("weights"):
        rows = jnp.concatenate([w_gate, w_up, w_down.T], axis=1)
        weights = lax.all_gather(rows, "dp", axis=0, tiled=True)

    with jax.named_scope("lookup"):
        local_ids = all_ids - lax.axis_index("tensor") * vocab_block
        inside = (local_ids >= 0) & (local_ids < vocab_block)
        picked = pick_rows(jnp.where(inside, local_ids, -1), pack_table(embed_table), feats)

    with jax.named_scope("embed_exchange"):
        blocks = picked.reshape(dp_count * tensor_count, part, tokens)
        blocks = lax.all_to_all(blocks, ("dp", "tensor"), 0, 0, tiled=True)
        blocks = blocks.reshape(dp_count, tensor_count, part, tokens)
        mine = jnp.sum(blocks.astype(jnp.float32), axis=1).astype(jnp.bfloat16)
        mine = mine.reshape(dp_count * part, tokens)
        embedded = gather_all(mine, "tensor")

    with jax.named_scope("forward"):
        sentences = 2 * pair_dev
        positions = jnp.arange(seq_len, dtype=jnp.int32)
        pad_mask = positions[None, :] < lengths.reshape(-1)[:, None]
        chosen_tokens = jnp.eye(16, sentences, dtype=jnp.bool_)[:, :, None] & pad_mask[None]
        chosen_tokens = chosen_tokens.reshape(16, tokens).astype(jnp.bfloat16)
        normed, activated, partial_out, resid_sum = forward(
            embedded, norm_gain[:, None], chosen_tokens, weights, units, feats, sentences
        )
        down = weights[:, 2 * units :]

    with jax.named_scope("pool"):
        seq_lens = lengths.reshape(-1).astype(jnp.float32)
        out_sum = jnp.sum(lax.all_to_all(partial_out, "tensor", 0, 0, tiled=True), axis=0)
        pooled = (resid_sum + out_sum) / seq_lens[:, None]
        inv_rms = lax.rsqrt(jnp.mean(pooled * pooled, axis=-1, keepdims=True) + 1e-06)
        reps = (pooled * inv_rms).astype(jnp.bfloat16)

    with jax.named_scope("scores"):
        half = width // 2
        halves = reps.reshape(2 * pair_dev, 2, half).transpose(1, 0, 2)
        halves = jnp.broadcast_to(halves[None], (dp_count // 2, 2, 2 * pair_dev, half))
        mine = lax.all_to_all(
            halves.reshape(dp_count, 2 * pair_dev, half), "dp", 0, 0, tiled=True
        )
        sides = [mine, lax.ppermute(mine, "dp", swap_cores)]
        queries = [side[:, :pair_dev].reshape(pair_total, half) for side in sides]
        passages = [side[:, pair_dev:].reshape(pair_total, half) for side in sides]
        factor = score_scale / width
        scores = factor * sum(product(q, p, 1, 1) for q, p in zip(queries, passages))
        log_total = jnp.log(jnp.sum(jnp.exp(scores), axis=1, keepdims=True))
        columns = jnp.arange(pair_total, dtype=jnp.int32)
        one_hot = (columns[None, :] == all_pos[:, None]).astype(jnp.float32)
        chosen = jnp.sum(scores * one_hot, axis=1, keepdims=True)
        loss = jnp.sum(log_total - chosen) / pair_total
        coef = (jnp.exp(scores - log_total) - one_hot).astype(jnp.bfloat16)
        first = lax.axis_index("dp") * pair_dev
        coef_rows = lax.dynamic_slice_in_dim(coef, first, pair_dev, 0)
        coef_columns = lax.dynamic_slice_in_dim(coef, first, pair_dev, 1)
        grads = [
            factor * jnp.concatenate([product(coef_rows, p, 1, 0), product(coef_columns, q, 0, 0)])
            for q, p in zip(queries, passages)
        ]
        grad_reps = jnp.where(
            even_core,
            jnp.concatenate([grads[0], grads[1]], axis=1),
            jnp.concatenate([grads[1], grads[0]], axis=1),
        )

    with jax.named_scope("backward"):
        grad_pooled = (
            inv_rms * grad_reps
            - pooled * inv_rms**3 * jnp.sum(grad_reps * pooled, axis=-1, keepdims=True) / width
        )
        token_grad = (grad_pooled / seq_lens[:, None]).astype(jnp.bfloat16)
        d_hidden = product(token_grad, down, 1, 0)
        d_tokens = jnp.where(pad_mask[:, :, None], d_hidden[:, None, :], 0.0).reshape(tokens, units)
        d_up = (d_tokens * activated).astype(jnp.bfloat16)
        by_core = normed.reshape(dp_count // 2, 2, feats, tokens)
        own_rows = jnp.where(even_core, by_core[:, 0], by_core[:, 1]).reshape(-1, tokens)
        other_rows = jnp.where(even_core, by_core[:, 1], by_core[:, 0]).reshape(-1, tokens)
        sent = product(other_rows, d_up, 1, 0).astype(jnp.bfloat16)
        got = lax.ppermute(sent, "dp", swap_cores)
        partial_grad = (product(own_rows, d_up, 1, 0) + got.astype(jnp.float32)).astype(jnp.bfloat16)
        same_core = [list(range(core, dp_count, 2)) for core in range(2)]
        parts = lax.all_to_all(
            partial_grad.reshape(dp_count // 2, feats, units),
            "dp",
            0,
            0,
            tiled=True,
            axis_index_groups=same_core,
        )
        grad_up = jnp.sum(parts.astype(jnp.float32), axis=0)
    return (loss, grad_up)


def solution(mesh):
    in_specs = (
        P(None, "dp", None),
        P(None, "dp"),
        P("dp"),
        P("dp", "tensor"),
        P(),
        P("dp", "tensor"),
        P("dp", "tensor"),
        P("tensor", "dp"),
    )
    out_specs = (P(), P("dp", "tensor"))
    return jax.shard_map(
        on_device, mesh=mesh, in_specs=in_specs, out_specs=out_specs, check_vma=False
    )
```

```python
import functools

import jax
import jax.numpy as jnp
from jax import lax
from jax.experimental import pallas as pl
from jax.experimental.pallas import tpu as pltpu
from jax.sharding import PartitionSpec as P

score_scale = 20.0
lanes = 128


def product(left, right, left_dim, right_dim):
    return lax.dot_general(
        left, right, (((left_dim,), (right_dim,)), ((), ())), preferred_element_type=jnp.float32
    )


def gather_all(block, axis):
    count = lax.axis_size(axis)
    copies = jnp.broadcast_to(block[None], (count,) + block.shape)
    return lax.all_to_all(copies, axis, 0, 0, tiled=True)


def ids_kernel(pos_ref, ids_ref, out_ref):
    sides, pair_dev, seq_len = ids_ref.shape
    ids = jnp.concatenate(
        [ids_ref[side, pl.ds(pair, 1), :] for side in range(sides) for pair in range(pair_dev)], axis=1
    )
    lane = lax.broadcasted_iota(jnp.int32, (1, lanes), 1)
    marks = jnp.zeros((1, lanes), jnp.int32)
    for pair in range(pair_dev):
        marks = jnp.where(lane == pair, pos_ref[pair], marks)
    rows = [ids[:, start : start + lanes] for start in range(0, ids.shape[1], lanes)] + [marks]
    out_ref[...] = jnp.broadcast_to(jnp.concatenate(rows, axis=0)[None], out_ref.shape)


def spread_ids(token_ids, positives, count):
    return pl.pallas_call(
        ids_kernel,
        out_shape=jax.ShapeDtypeStruct((count, token_ids.size // lanes + 1, lanes), jnp.int32),
        in_specs=[pl.BlockSpec(memory_space=pltpu.SMEM), pl.BlockSpec(memory_space=pltpu.VMEM)],
        out_specs=pl.BlockSpec(memory_space=pltpu.VMEM),
    )(positives, token_ids)


def pack_kernel(span, table_ref, rows_ref):
    feats, vocab = table_ref.shape
    slots = lanes // feats

    def piece(slot, start, wide):
        return table_ref[:, pl.ds(slot * span + start, wide)].astype(jnp.float32)

    whole = (vocab - (slots - 1) * span) // lanes

    @pl.loop(0, whole)
    def _(step):
        start = pl.multiple_of(step * lanes, lanes)
        stacked = jnp.concatenate([piece(slot, start, lanes) for slot in range(slots)], axis=0)
        rows_ref[pl.ds(start, lanes), 0, :] = stacked.T

    for step in range(whole, span // lanes):
        start = step * lanes
        left = max(0, vocab - (slots - 1) * span - start)
        last = jnp.zeros((feats, lanes - left), jnp.float32)
        if left:
            last = jnp.concatenate([piece(slots - 1, start, left), last], axis=1)
        stacked = jnp.concatenate([piece(slot, start, lanes) for slot in range(slots - 1)] + [last], axis=0)
        rows_ref[start : start + lanes, 0, :] = stacked.T


def pick_kernel(chunks, row_ref, slot_ref, rows_ref, out_ref, even_ref, odd_ref, near_ref, sems):
    groups, tokens = row_ref.shape
    feats = out_ref.shape[1]
    slots = lanes // feats
    chunk = groups // chunks

    def bring(index):
        where = pl.ds(index * chunk, chunk)
        return pltpu.make_async_copy(row_ref.at[where], near_ref.at[where], sems.at[index])

    def read(group, held_ref):
        for token in range(tokens):
            held_ref[pl.ds(token, 1), :] = rows_ref[near_ref[group, token]]

    def turn(group, held_ref):
        slot = slot_ref[pl.ds(group, 1), :]
        for first in range(0, tokens, lanes):
            turned = held_ref[first : first + lanes, :].T
            mine = slot[:, first : first + lanes]
            total = jnp.zeros((feats, lanes), jnp.float32)
            for part in range(slots):
                total = jnp.where(mine == part, turned[part * feats : (part + 1) * feats], total)
            out_ref[group, :, first : first + lanes] = total.astype(out_ref.dtype)

    for index in range(chunks):
        bring(index).start()
    bring(0).wait()
    read(0, even_ref)

    @pl.loop(0, groups // 2)
    def _(step):
        ahead = step * 2 // chunk + 1

        @pl.when((step * 2 % chunk == 0) & (ahead < chunks))
        def _():
            bring(ahead).wait()

        read(step * 2 + 1, odd_ref)
        turn(step * 2, even_ref)
        read(jnp.minimum(step * 2 + 2, groups - 1), even_ref)
        turn(step * 2 + 1, odd_ref)


def pack_table(table):
    feats, vocab = table.shape
    slots = lanes // feats
    span = -(-vocab // (slots * lanes)) * lanes
    return pl.pallas_call(
        functools.partial(pack_kernel, span),
        out_shape=jax.ShapeDtypeStruct((span, 1, lanes), jnp.float32),
        in_specs=[pl.BlockSpec(memory_space=pltpu.VMEM)],
        out_specs=pl.BlockSpec(memory_space=pltpu.VMEM),
        compiler_params=pltpu.CompilerParams(vmem_limit_bytes=10 << 20),
        cost_estimate=pl.CostEstimate(flops=0, bytes_accessed=20 << 20, transcendentals=0),
    )(table)


def pick_rows(rows, packed, feats):
    slots = lanes // feats
    span = packed.shape[0]
    groups, tokens = rows.shape
    chunks = 8 if groups % 16 == 0 else 1
    inside = (rows >= 0) & (rows < slots * span)
    safe = jnp.where(inside, rows, 0)
    slot = safe // span
    row = safe - slot * span
    slot = jnp.where(inside, slot, slots)
    return pl.pallas_call(
        functools.partial(pick_kernel, chunks),
        out_shape=jax.ShapeDtypeStruct((groups, feats, tokens), jnp.bfloat16),
        in_specs=[pl.BlockSpec(memory_space=pltpu.VMEM)] * 3,
        out_specs=pl.BlockSpec(memory_space=pltpu.VMEM),
        scratch_shapes=[
            pltpu.VMEM((tokens, lanes), jnp.float32),
            pltpu.VMEM((tokens, lanes), jnp.float32),
            pltpu.SMEM((groups, tokens), jnp.int32),
            pltpu.SemaphoreType.DMA((chunks,)),
        ],
        compiler_params=pltpu.CompilerParams(vmem_limit_bytes=10 << 20),
        cost_estimate=pl.CostEstimate(flops=0, bytes_accessed=30 << 20, transcendentals=0),
    )(row, slot, packed)


def gelu(v):
    return 0.5 * v * (1.0 + jnp.tanh(0.7978845608028654 * (v + 0.044715 * (v * v * v))))


def forward_kernel(
    units,
    feats,
    x_ref,
    gain_ref,
    mask_ref,
    weights_ref,
    normed_ref,
    act_ref,
    out_ref,
    sum_ref,
    resid_ref,
    wide_ref,
    down_ref,
    total_ref,
    pool_ref,
    sems,
):
    bring_wide = pltpu.make_async_copy(weights_ref.at[:, pl.ds(0, 2 * units)], wide_ref, sems.at[0])
    bring_down = pltpu.make_async_copy(weights_ref.at[:, pl.ds(2 * units, units)], down_ref, sems.at[1])
    bring_wide.start()
    bring_down.start()
    parts, part_rows, tokens = x_ref.shape
    part = feats // parts
    for index in range(parts):
        rows = x_ref[index].astype(jnp.float32)
        for block in range(part_rows // part):
            start = block * feats + index * part
            resid_ref[start : start + part, :] = rows[block * part : (block + 1) * part]
    resid = resid_ref[...]
    scale = lax.rsqrt(jnp.mean(resid * resid, axis=0, keepdims=True) + 1e-06)
    normed_ref[...] = (resid * scale * gain_ref[...]).astype(jnp.bfloat16)
    mask = mask_ref[...]
    first = (((0,), (0,)), ((), ()))
    last = (((1,), (1,)), ((), ()))
    sentences = sum_ref.shape[0]
    pool_ref[...] = lax.dot_general(
        mask, resid.astype(jnp.bfloat16), last, preferred_element_type=jnp.float32
    )[:sentences]
    keep_sum = pltpu.make_async_copy(pool_ref, sum_ref, sems.at[2])
    keep_sum.start()
    bring_wide.wait()
    both = lax.dot_general(normed_ref[...], wide_ref[...], first, preferred_element_type=jnp.float32)
    act = gelu(both[:, :units])
    act_ref[...] = act
    hidden = (act * both[:, units:]).astype(jnp.bfloat16)
    hidden_sum = jnp.dot(mask, hidden, preferred_element_type=jnp.float32)
    high = hidden_sum.astype(jnp.bfloat16)
    low = (hidden_sum - high.astype(jnp.float32)).astype(jnp.bfloat16)
    bring_down.wait()
    terms = lax.dot_general(
        jnp.concatenate([high, low], axis=0), down_ref[...], last, preferred_element_type=jnp.float32
    )
    rows = mask.shape[0]
    total_ref[...] = (terms[:rows] + terms[rows:])[:sentences]
    copies = [
        pltpu.make_async_copy(total_ref, out_ref.at[index], sems.at[3 + index]) for index in range(parts)
    ]
    for copy in copies:
        copy.start()
    for copy in copies:
        copy.wait()
    keep_sum.wait()


def forward(embedded, gain, mask, weights, units, feats, sentences):
    count, part_rows, tokens = embedded.shape
    width = count * part_rows
    vmem, here = pl.BlockSpec(memory_space=pltpu.VMEM), pl.BlockSpec(memory_space=pl.ANY)
    return pl.pallas_call(
        functools.partial(forward_kernel, units, feats),
        out_shape=[
            jax.ShapeDtypeStruct((width, tokens), jnp.bfloat16),
            jax.ShapeDtypeStruct((tokens, units), jnp.float32),
            jax.ShapeDtypeStruct((count, sentences, width), jnp.float32),
            jax.ShapeDtypeStruct((sentences, width), jnp.float32),
        ],
        in_specs=[vmem, vmem, vmem, here],
        out_specs=[vmem, vmem, here, here],
        scratch_shapes=[
            pltpu.VMEM((width, tokens), jnp.float32),
            pltpu.VMEM((width, 2 * units), jnp.bfloat16),
            pltpu.VMEM((width, units), jnp.bfloat16),
            pltpu.VMEM((sentences, width), jnp.float32),
            pltpu.VMEM((sentences, width), jnp.float32),
            pltpu.SemaphoreType.DMA((3 + count,)),
        ],
        compiler_params=pltpu.CompilerParams(vmem_limit_bytes=24 << 20),
        cost_estimate=pl.CostEstimate(
            flops=6 * width * tokens * units, bytes_accessed=10 << 20, transcendentals=tokens * units
        ),
    )(embedded, gain, mask, weights)


def on_device(token_ids, lengths, positives, embed_table, norm_gain, w_gate, w_up, w_down):
    dp_count = lax.axis_size("dp")
    tensor_count = lax.axis_size("tensor")
    pair_dev = token_ids.shape[1]
    seq_len = token_ids.shape[2]
    feats, vocab_block = embed_table.shape
    width = feats * dp_count
    units = w_gate.shape[1]
    pair_total = pair_dev * dp_count
    tokens = 2 * pair_dev * seq_len
    part = feats // tensor_count
    even_core = lax.axis_index("dp") % 2 == 0
    swap_cores = [(index, index ^ 1) for index in range(dp_count)]

    with jax.named_scope("ids"):
        spread = spread_ids(token_ids, positives, dp_count)
        spread, w_gate, w_up, w_down = lax.optimization_barrier((spread, w_gate, w_up, w_down))
        arrived = lax.all_to_all(spread, "dp", 0, 0, tiled=True)
        all_ids = arrived[:, : tokens // lanes].reshape(dp_count, tokens)
        all_pos = arrived[:, tokens // lanes, :pair_dev].reshape(-1)

    with jax.named_scope("weights"):
        rows = jnp.concatenate([w_gate, w_up, w_down.T], axis=1)
        weights = lax.all_gather(rows, "dp", axis=0, tiled=True)

    with jax.named_scope("lookup"):
        local_ids = all_ids - lax.axis_index("tensor") * vocab_block
        inside = (local_ids >= 0) & (local_ids < vocab_block)
        picked = pick_rows(jnp.where(inside, local_ids, -1), pack_table(embed_table), feats)

    with jax.named_scope("embed_exchange"):
        blocks = picked.reshape(dp_count * tensor_count, part, tokens)
        blocks = lax.all_to_all(blocks, ("dp", "tensor"), 0, 0, tiled=True)
        blocks = blocks.reshape(dp_count, tensor_count, part, tokens)
        mine = jnp.sum(blocks.astype(jnp.float32), axis=1).astype(jnp.bfloat16)
        mine = mine.reshape(dp_count * part, tokens)
        embedded = gather_all(mine, "tensor")

    with jax.named_scope("forward"):
        sentences = 2 * pair_dev
        positions = jnp.arange(seq_len, dtype=jnp.int32)
        pad_mask = positions[None, :] < lengths.reshape(-1)[:, None]
        chosen_tokens = jnp.eye(16, sentences, dtype=jnp.bool_)[:, :, None] & pad_mask[None]
        chosen_tokens = chosen_tokens.reshape(16, tokens).astype(jnp.bfloat16)
        normed, activated, partial_out, resid_sum = forward(
            embedded, norm_gain[:, None], chosen_tokens, weights, units, feats, sentences
        )
        down = weights[:, 2 * units :]

    with jax.named_scope("pool"):
        seq_lens = lengths.reshape(-1).astype(jnp.float32)
        out_sum = jnp.sum(lax.all_to_all(partial_out, "tensor", 0, 0, tiled=True), axis=0)
        pooled = (resid_sum + out_sum) / seq_lens[:, None]
        inv_rms = lax.rsqrt(jnp.mean(pooled * pooled, axis=-1, keepdims=True) + 1e-06)
        reps = (pooled * inv_rms).astype(jnp.bfloat16)

    with jax.named_scope("scores"):
        half = width // 2
        halves = reps.reshape(2 * pair_dev, 2, half).transpose(1, 0, 2)
        halves = jnp.broadcast_to(halves[None], (dp_count // 2, 2, 2 * pair_dev, half))
        mine = lax.all_to_all(
            halves.reshape(dp_count, 2 * pair_dev, half), "dp", 0, 0, tiled=True
        )
        sides = [mine, lax.ppermute(mine, "dp", swap_cores)]
        queries = [side[:, :pair_dev].reshape(pair_total, half) for side in sides]
        passages = [side[:, pair_dev:].reshape(pair_total, half) for side in sides]
        factor = score_scale / width
        scores = factor * sum(product(q, p, 1, 1) for q, p in zip(queries, passages))
        log_total = jnp.log(jnp.sum(jnp.exp(scores), axis=1, keepdims=True))
        columns = jnp.arange(pair_total, dtype=jnp.int32)
        one_hot = (columns[None, :] == all_pos[:, None]).astype(jnp.float32)
        chosen = jnp.sum(scores * one_hot, axis=1, keepdims=True)
        loss = jnp.sum(log_total - chosen) / pair_total
        coef = (jnp.exp(scores - log_total) - one_hot).astype(jnp.bfloat16)
        first = lax.axis_index("dp") * pair_dev
        coef_rows = lax.dynamic_slice_in_dim(coef, first, pair_dev, 0)
        coef_columns = lax.dynamic_slice_in_dim(coef, first, pair_dev, 1)
        grads = [
            factor * jnp.concatenate([product(coef_rows, p, 1, 0), product(coef_columns, q, 0, 0)])
            for q, p in zip(queries, passages)
        ]
        grad_reps = jnp.where(
            even_core,
            jnp.concatenate([grads[0], grads[1]], axis=1),
            jnp.concatenate([grads[1], grads[0]], axis=1),
        )

    with jax.named_scope("backward"):
        grad_pooled = (
            inv_rms * grad_reps
            - pooled * inv_rms**3 * jnp.sum(grad_reps * pooled, axis=-1, keepdims=True) / width
        )
        token_grad = (grad_pooled / seq_lens[:, None]).astype(jnp.bfloat16)
        d_hidden = product(token_grad, down, 1, 0)
        d_tokens = jnp.where(pad_mask[:, :, None], d_hidden[:, None, :], 0.0).reshape(tokens, units)
        d_up = (d_tokens * activated).astype(jnp.bfloat16)
        by_core = normed.reshape(dp_count // 2, 2, feats, tokens)
        own_rows = jnp.where(even_core, by_core[:, 0], by_core[:, 1]).reshape(-1, tokens)
        other_rows = jnp.where(even_core, by_core[:, 1], by_core[:, 0]).reshape(-1, tokens)
        sent = product(other_rows, d_up, 1, 0).astype(jnp.bfloat16)
        got = lax.ppermute(sent, "dp", swap_cores)
        partial_grad = (product(own_rows, d_up, 1, 0) + got.astype(jnp.float32)).astype(jnp.bfloat16)
        same_core = [list(range(core, dp_count, 2)) for core in range(2)]
        parts = lax.all_to_all(
            partial_grad.reshape(dp_count // 2, feats, units),
            "dp",
            0,
            0,
            tiled=True,
            axis_index_groups=same_core,
        )
        grad_up = jnp.sum(parts.astype(jnp.float32), axis=0)
    return (loss, grad_up)


def solution(mesh):
    in_specs = (
        P(None, "dp", None),
        P(None, "dp"),
        P("dp"),
        P("dp", "tensor"),
        P(),
        P("dp", "tensor"),
        P("dp", "tensor"),
        P("tensor", "dp"),
    )
    out_specs = (P(), P("dp", "tensor"))
    return jax.shard_map(
        on_device, mesh=mesh, in_specs=in_specs, out_specs=out_specs, check_vma=False
    )
```

```python
import functools

import jax
import jax.numpy as jnp
from jax import lax
from jax.experimental import pallas as pl
from jax.experimental.pallas import tpu as pltpu
from jax.sharding import PartitionSpec as P

score_scale = 20.0
lanes = 128


def product(left, right, left_dim, right_dim):
    return lax.dot_general(
        left, right, (((left_dim,), (right_dim,)), ((), ())), preferred_element_type=jnp.float32
    )


def gather_all(block, axis):
    count = lax.axis_size(axis)
    copies = jnp.broadcast_to(block[None], (count,) + block.shape)
    return lax.all_to_all(copies, axis, 0, 0, tiled=True)


def ids_kernel(pos_ref, ids_ref, out_ref):
    sides, pair_dev, seq_len = ids_ref.shape
    ids = jnp.concatenate(
        [ids_ref[side, pl.ds(pair, 1), :] for side in range(sides) for pair in range(pair_dev)], axis=1
    )
    lane = lax.broadcasted_iota(jnp.int32, (1, lanes), 1)
    marks = jnp.zeros((1, lanes), jnp.int32)
    for pair in range(pair_dev):
        marks = jnp.where(lane == pair, pos_ref[pair], marks)
    rows = [ids[:, start : start + lanes] for start in range(0, ids.shape[1], lanes)] + [marks]
    out_ref[...] = jnp.broadcast_to(jnp.concatenate(rows, axis=0)[None], out_ref.shape)


def spread_ids(token_ids, positives, count):
    return pl.pallas_call(
        ids_kernel,
        out_shape=jax.ShapeDtypeStruct((count, token_ids.size // lanes + 1, lanes), jnp.int32),
        in_specs=[pl.BlockSpec(memory_space=pltpu.SMEM), pl.BlockSpec(memory_space=pltpu.VMEM)],
        out_specs=pl.BlockSpec(memory_space=pltpu.VMEM),
    )(positives, token_ids)


def pack_kernel(span, table_ref, rows_ref):
    feats, vocab = table_ref.shape
    slots = lanes // feats

    def piece(slot, start, wide):
        return table_ref[:, pl.ds(slot * span + start, wide)].astype(jnp.float32)

    whole = (vocab - (slots - 1) * span) // lanes

    @pl.loop(0, whole)
    def _(step):
        start = pl.multiple_of(step * lanes, lanes)
        stacked = jnp.concatenate([piece(slot, start, lanes) for slot in range(slots)], axis=0)
        rows_ref[pl.ds(start, lanes), 0, :] = stacked.T

    for step in range(whole, span // lanes):
        start = step * lanes
        left = max(0, vocab - (slots - 1) * span - start)
        last = jnp.zeros((feats, lanes - left), jnp.float32)
        if left:
            last = jnp.concatenate([piece(slots - 1, start, left), last], axis=1)
        stacked = jnp.concatenate([piece(slot, start, lanes) for slot in range(slots - 1)] + [last], axis=0)
        rows_ref[start : start + lanes, 0, :] = stacked.T


def pick_kernel(chunks, row_ref, slot_ref, rows_ref, out_ref, even_ref, odd_ref, near_ref, sems):
    groups, tokens = row_ref.shape
    feats = out_ref.shape[1]
    slots = lanes // feats
    chunk = groups // chunks

    def bring(index):
        where = pl.ds(index * chunk, chunk)
        return pltpu.make_async_copy(row_ref.at[where], near_ref.at[where], sems.at[index])

    def read(group, held_ref):
        for token in range(tokens):
            held_ref[pl.ds(token, 1), :] = rows_ref[near_ref[group, token]]

    def turn(group, held_ref):
        slot = slot_ref[pl.ds(group, 1), :]
        for first in range(0, tokens, lanes):
            turned = held_ref[first : first + lanes, :].T
            mine = slot[:, first : first + lanes]
            total = jnp.zeros((feats, lanes), jnp.float32)
            for part in range(slots):
                total = jnp.where(mine == part, turned[part * feats : (part + 1) * feats], total)
            out_ref[group, :, first : first + lanes] = total.astype(out_ref.dtype)

    for index in range(chunks):
        bring(index).start()
    bring(0).wait()
    read(0, even_ref)

    @pl.loop(0, groups // 2)
    def _(step):
        ahead = step * 2 // chunk + 1

        @pl.when((step * 2 % chunk == 0) & (ahead < chunks))
        def _():
            bring(ahead).wait()

        read(step * 2 + 1, odd_ref)
        turn(step * 2, even_ref)
        read(jnp.minimum(step * 2 + 2, groups - 1), even_ref)
        turn(step * 2 + 1, odd_ref)


def pack_table(table):
    feats, vocab = table.shape
    slots = lanes // feats
    span = -(-vocab // (slots * lanes)) * lanes
    return pl.pallas_call(
        functools.partial(pack_kernel, span),
        out_shape=jax.ShapeDtypeStruct((span, 1, lanes), jnp.float32),
        in_specs=[pl.BlockSpec(memory_space=pltpu.VMEM)],
        out_specs=pl.BlockSpec(memory_space=pltpu.VMEM),
        compiler_params=pltpu.CompilerParams(vmem_limit_bytes=10 << 20),
        cost_estimate=pl.CostEstimate(flops=0, bytes_accessed=20 << 20, transcendentals=0),
    )(table)


def pick_rows(rows, packed, feats):
    slots = lanes // feats
    span = packed.shape[0]
    groups, tokens = rows.shape
    chunks = 8 if groups % 16 == 0 else 1
    inside = (rows >= 0) & (rows < slots * span)
    safe = jnp.where(inside, rows, 0)
    slot = safe // span
    row = safe - slot * span
    slot = jnp.where(inside, slot, slots)
    return pl.pallas_call(
        functools.partial(pick_kernel, chunks),
        out_shape=jax.ShapeDtypeStruct((groups, feats, tokens), jnp.bfloat16),
        in_specs=[pl.BlockSpec(memory_space=pltpu.VMEM)] * 3,
        out_specs=pl.BlockSpec(memory_space=pltpu.VMEM),
        scratch_shapes=[
            pltpu.VMEM((tokens, lanes), jnp.float32),
            pltpu.VMEM((tokens, lanes), jnp.float32),
            pltpu.SMEM((groups, tokens), jnp.int32),
            pltpu.SemaphoreType.DMA((chunks,)),
        ],
        compiler_params=pltpu.CompilerParams(vmem_limit_bytes=10 << 20),
        cost_estimate=pl.CostEstimate(flops=0, bytes_accessed=30 << 20, transcendentals=0),
    )(row, slot, packed)


def gelu(v):
    return 0.5 * v * (1.0 + jnp.tanh(0.7978845608028654 * (v + 0.044715 * (v * v * v))))


def forward_kernel(
    units,
    feats,
    x_ref,
    gain_ref,
    mask_ref,
    weights_ref,
    normed_ref,
    act_ref,
    out_ref,
    sum_ref,
    resid_ref,
    wide_ref,
    down_ref,
    total_ref,
    pool_ref,
    sems,
):
    bring_wide = pltpu.make_async_copy(weights_ref.at[:, pl.ds(0, 2 * units)], wide_ref, sems.at[0])
    bring_down = pltpu.make_async_copy(weights_ref.at[:, pl.ds(2 * units, units)], down_ref, sems.at[1])
    bring_wide.start()
    bring_down.start()
    parts, part_rows, tokens = x_ref.shape
    part = feats // parts
    for index in range(parts):
        rows = x_ref[index].astype(jnp.float32)
        for block in range(part_rows // part):
            start = block * feats + index * part
            resid_ref[start : start + part, :] = rows[block * part : (block + 1) * part]
    resid = resid_ref[...]
    scale = lax.rsqrt(jnp.mean(resid * resid, axis=0, keepdims=True) + 1e-06)
    normed_ref[...] = (resid * scale * gain_ref[...]).astype(jnp.bfloat16)
    mask = mask_ref[...]
    first = (((0,), (0,)), ((), ()))
    last = (((1,), (1,)), ((), ()))
    sentences = sum_ref.shape[0]
    pool_ref[...] = lax.dot_general(
        mask, resid.astype(jnp.bfloat16), last, preferred_element_type=jnp.float32
    )[:sentences]
    keep_sum = pltpu.make_async_copy(pool_ref, sum_ref, sems.at[2])
    keep_sum.start()
    bring_wide.wait()
    both = lax.dot_general(normed_ref[...], wide_ref[...], first, preferred_element_type=jnp.float32)
    act = gelu(both[:, :units])
    act_ref[...] = act
    hidden = (act * both[:, units:]).astype(jnp.bfloat16)
    hidden_sum = jnp.dot(mask, hidden, preferred_element_type=jnp.float32)
    high = hidden_sum.astype(jnp.bfloat16)
    low = (hidden_sum - high.astype(jnp.float32)).astype(jnp.bfloat16)
    bring_down.wait()
    terms = lax.dot_general(
        jnp.concatenate([high, low], axis=0), down_ref[...], last, preferred_element_type=jnp.float32
    )
    rows = mask.shape[0]
    total_ref[...] = (terms[:rows] + terms[rows:])[:sentences]
    copies = [
        pltpu.make_async_copy(total_ref, out_ref.at[index], sems.at[3 + index]) for index in range(parts)
    ]
    for copy in copies:
        copy.start()
    for copy in copies:
        copy.wait()
    keep_sum.wait()


def forward(embedded, gain, mask, weights, units, feats, sentences):
    count, part_rows, tokens = embedded.shape
    width = count * part_rows
    vmem, here = pl.BlockSpec(memory_space=pltpu.VMEM), pl.BlockSpec(memory_space=pl.ANY)
    return pl.pallas_call(
        functools.partial(forward_kernel, units, feats),
        out_shape=[
            jax.ShapeDtypeStruct((width, tokens), jnp.bfloat16),
            jax.ShapeDtypeStruct((tokens, units), jnp.float32),
            jax.ShapeDtypeStruct((count, sentences, width), jnp.float32),
            jax.ShapeDtypeStruct((sentences, width), jnp.float32),
        ],
        in_specs=[vmem, vmem, vmem, here],
        out_specs=[vmem, vmem, here, here],
        scratch_shapes=[
            pltpu.VMEM((width, tokens), jnp.float32),
            pltpu.VMEM((width, 2 * units), jnp.bfloat16),
            pltpu.VMEM((width, units), jnp.bfloat16),
            pltpu.VMEM((sentences, width), jnp.float32),
            pltpu.VMEM((sentences, width), jnp.float32),
            pltpu.SemaphoreType.DMA((3 + count,)),
        ],
        compiler_params=pltpu.CompilerParams(vmem_limit_bytes=24 << 20),
        cost_estimate=pl.CostEstimate(
            flops=6 * width * tokens * units, bytes_accessed=10 << 20, transcendentals=tokens * units
        ),
    )(embedded, gain, mask, weights)


def on_device(token_ids, lengths, positives, embed_table, norm_gain, w_gate, w_up, w_down):
    dp_count = lax.axis_size("dp")
    tensor_count = lax.axis_size("tensor")
    pair_dev = token_ids.shape[1]
    seq_len = token_ids.shape[2]
    feats, vocab_block = embed_table.shape
    width = feats * dp_count
    units = w_gate.shape[1]
    pair_total = pair_dev * dp_count
    tokens = 2 * pair_dev * seq_len
    part = feats // tensor_count
    even_core = lax.axis_index("dp") % 2 == 0
    swap_cores = [(index, index ^ 1) for index in range(dp_count)]

    with jax.named_scope("ids"):
        spread = spread_ids(token_ids, positives, dp_count)
        arrived = lax.all_to_all(spread, "dp", 0, 0, tiled=True)
        arrived, w_gate, w_up, w_down = lax.optimization_barrier((arrived, w_gate, w_up, w_down))
        all_ids = arrived[:, : tokens // lanes].reshape(dp_count, tokens)
        all_pos = arrived[:, tokens // lanes, :pair_dev].reshape(-1)

    with jax.named_scope("weights"):
        rows = jnp.concatenate([w_gate, w_up, w_down.T], axis=1)
        weights = lax.all_gather(rows, "dp", axis=0, tiled=True)

    with jax.named_scope("lookup"):
        local_ids = all_ids - lax.axis_index("tensor") * vocab_block
        inside = (local_ids >= 0) & (local_ids < vocab_block)
        picked = pick_rows(jnp.where(inside, local_ids, -1), pack_table(embed_table), feats)

    with jax.named_scope("embed_exchange"):
        blocks = picked.reshape(dp_count * tensor_count, part, tokens)
        blocks = lax.all_to_all(blocks, ("dp", "tensor"), 0, 0, tiled=True)
        blocks = blocks.reshape(dp_count, tensor_count, part, tokens)
        mine = jnp.sum(blocks.astype(jnp.float32), axis=1).astype(jnp.bfloat16)
        mine = mine.reshape(dp_count * part, tokens)
        embedded = gather_all(mine, "tensor")

    with jax.named_scope("forward"):
        sentences = 2 * pair_dev
        positions = jnp.arange(seq_len, dtype=jnp.int32)
        pad_mask = positions[None, :] < lengths.reshape(-1)[:, None]
        chosen_tokens = jnp.eye(16, sentences, dtype=jnp.bool_)[:, :, None] & pad_mask[None]
        chosen_tokens = chosen_tokens.reshape(16, tokens).astype(jnp.bfloat16)
        normed, activated, partial_out, resid_sum = forward(
            embedded, norm_gain[:, None], chosen_tokens, weights, units, feats, sentences
        )
        down = weights[:, 2 * units :]

    with jax.named_scope("pool"):
        seq_lens = lengths.reshape(-1).astype(jnp.float32)
        out_sum = jnp.sum(lax.all_to_all(partial_out, "tensor", 0, 0, tiled=True), axis=0)
        pooled = (resid_sum + out_sum) / seq_lens[:, None]
        inv_rms = lax.rsqrt(jnp.mean(pooled * pooled, axis=-1, keepdims=True) + 1e-06)
        reps = (pooled * inv_rms).astype(jnp.bfloat16)

    with jax.named_scope("scores"):
        half = width // 2
        halves = reps.reshape(2 * pair_dev, 2, half).transpose(1, 0, 2)
        halves = jnp.broadcast_to(halves[None], (dp_count // 2, 2, 2 * pair_dev, half))
        mine = lax.all_to_all(
            halves.reshape(dp_count, 2 * pair_dev, half), "dp", 0, 0, tiled=True
        )
        sides = [mine, lax.ppermute(mine, "dp", swap_cores)]
        queries = [side[:, :pair_dev].reshape(pair_total, half) for side in sides]
        passages = [side[:, pair_dev:].reshape(pair_total, half) for side in sides]
        factor = score_scale / width
        scores = factor * sum(product(q, p, 1, 1) for q, p in zip(queries, passages))
        log_total = jnp.log(jnp.sum(jnp.exp(scores), axis=1, keepdims=True))
        columns = jnp.arange(pair_total, dtype=jnp.int32)
        one_hot = (columns[None, :] == all_pos[:, None]).astype(jnp.float32)
        chosen = jnp.sum(scores * one_hot, axis=1, keepdims=True)
        loss = jnp.sum(log_total - chosen) / pair_total
        coef = (jnp.exp(scores - log_total) - one_hot).astype(jnp.bfloat16)
        first = lax.axis_index("dp") * pair_dev
        coef_rows = lax.dynamic_slice_in_dim(coef, first, pair_dev, 0)
        coef_columns = lax.dynamic_slice_in_dim(coef, first, pair_dev, 1)
        grads = [
            factor * jnp.concatenate([product(coef_rows, p, 1, 0), product(coef_columns, q, 0, 0)])
            for q, p in zip(queries, passages)
        ]
        grad_reps = jnp.where(
            even_core,
            jnp.concatenate([grads[0], grads[1]], axis=1),
            jnp.concatenate([grads[1], grads[0]], axis=1),
        )

    with jax.named_scope("backward"):
        grad_pooled = (
            inv_rms * grad_reps
            - pooled * inv_rms**3 * jnp.sum(grad_reps * pooled, axis=-1, keepdims=True) / width
        )
        token_grad = (grad_pooled / seq_lens[:, None]).astype(jnp.bfloat16)
        d_hidden = product(token_grad, down, 1, 0)
        d_tokens = jnp.where(pad_mask[:, :, None], d_hidden[:, None, :], 0.0).reshape(tokens, units)
        d_up = (d_tokens * activated).astype(jnp.bfloat16)
        by_core = normed.reshape(dp_count // 2, 2, feats, tokens)
        own_rows = jnp.where(even_core, by_core[:, 0], by_core[:, 1]).reshape(-1, tokens)
        other_rows = jnp.where(even_core, by_core[:, 1], by_core[:, 0]).reshape(-1, tokens)
        sent = product(other_rows, d_up, 1, 0).astype(jnp.bfloat16)
        got = lax.ppermute(sent, "dp", swap_cores)
        partial_grad = (product(own_rows, d_up, 1, 0) + got.astype(jnp.float32)).astype(jnp.bfloat16)
        same_core = [list(range(core, dp_count, 2)) for core in range(2)]
        parts = lax.all_to_all(
            partial_grad.reshape(dp_count // 2, feats, units),
            "dp",
            0,
            0,
            tiled=True,
            axis_index_groups=same_core,
        )
        grad_up = jnp.sum(parts.astype(jnp.float32), axis=0)
    return (loss, grad_up)


def solution(mesh):
    in_specs = (
        P(None, "dp", None),
        P(None, "dp"),
        P("dp"),
        P("dp", "tensor"),
        P(),
        P("dp", "tensor"),
        P("dp", "tensor"),
        P("tensor", "dp"),
    )
    out_specs = (P(), P("dp", "tensor"))
    return jax.shard_map(
        on_device, mesh=mesh, in_specs=in_specs, out_specs=out_specs, check_vma=False
    )
```
